128 devices in a mesh: seq: 16 (over x_hi, y, core), head: 8 (over z, x_lo).
Axes of the slice: x: 4 (x_hi: 2, x_lo: 2; x = x_hi * 2 + x_lo), y: 4, z: 4, core: 2. Of those that a mesh axis runs over, the one named last changes fastest.
Arguments:
- prompt_k: bfloat16 [5120, 1024], P(('seq', 'head')), may hold values from -6 to 6
- prompt_v: bfloat16 [5120, 1024], P(('seq', 'head')), may hold values from -6 to 6
- resp_q: bfloat16 [4096, 8192], P('seq', 'head'), may hold values from -7 to 7
- resp_k: bfloat16 [4096, 1024], P('seq', 'head'), may hold values from -6 to 6
- resp_v: bfloat16 [4096, 1024], P('seq', 'head'), may hold values from -6 to 6
- grad_out: bfloat16 [4096, 8192], P('seq', 'head'), may hold values from -6 to 6
- resp_lengths: int32 [8], replicated, may hold values from 1 to 1024, 4096 in all
Outputs:
- resp_out: bfloat16 [4096, 8192], P('seq', 'head')
- grad_q: bfloat16 [4096, 8192], P('seq', 'head')
- grad_k_resp: bfloat16 [4096, 1024], P('seq', 'head')
- grad_v_resp: bfloat16 [4096, 1024], P('seq', 'head')
- grad_k_prompt: bfloat16 [5120, 1024], P(('seq', 'head'))
- grad_v_prompt: bfloat16 [5120, 1024], P(('seq', 'head'))
The draws below stay inside these ranges and needn't reach their ends.
Inputs may be any that keep to these rules, and one draw needn't show every extreme that they name: `resp_lengths`: the 8 lengths add up to 4096, and the largest is exactly 1024.
All inputs are finite; a program needn't handle non-finite values.
Results may differ from the reference program's by a relative error of at most 0.02.
Values may be sent and summed in bfloat16 or wider, within the bound.
A program may use at most 128 MiB of HBM per device.

```python
import math
import jax
import jax.numpy as jnp
import numpy as np
from jax import lax

H = 64
KVH = 8
HD = 128
NRESP = 8
P_SIZE = 5120
R = 4096
LMAX = 1024


def draw_resp_q(key, part):
    key = jax.random.fold_in(key, 1)
    values = jax.random.truncated_normal(key, -6.0, 6.0, (R, H, HD), jnp.float32)
    return values.reshape(R, H * HD).astype(jnp.bfloat16)


def draw_prompt_k(key, part):
    key = jax.random.fold_in(key, 2)
    values = jax.random.truncated_normal(key, -6.0, 6.0, (P_SIZE, KVH, HD), jnp.float32)
    return values.reshape(P_SIZE, KVH * HD).astype(jnp.bfloat16)


def block_scale(stream_key, extent, split, smallest, high):
    level = 1.0
    for axis_at, blocks in split:
        heights = jax.random.uniform(jax.random.fold_in(jax.random.fold_in(stream_key, 6), axis_at), (blocks,), jnp.float32, smallest / len(split), high / len(split))
        level = level * jnp.repeat(jnp.exp(heights), extent[axis_at] // blocks).reshape((-1,) + (1,) * (len(extent) - 1 - axis_at))
    return level


def length_profile(amount, total, reach, lean):
    weights = [(1 << 20) // math.isqrt(grade ** lean) + 1 for grade in range(2, amount + 1)]
    rest, given = total - reach - (amount - 1), [1] * (amount - 1)
    while rest > 0:
        movable = [i for i in range(amount - 1) if given[i] < reach]
        pool, left = sum([weights[i] for i in movable]), rest
        for i in movable:
            extra = min(reach - given[i], max(1, left * weights[i] // pool), rest)
            given[i] = given[i] + extra
            rest = rest - extra
    return np.array([reach] + given)


def uneven(rng, count, total, limit, lean):
    if count == 2:
        one = jax.random.randint(rng, (), max(1, total - limit), min(limit, total - 1) + 1)
        return jnp.stack([one, total - one])
    lengths = jnp.asarray(length_profile(count, total, limit, lean), jnp.int32)
    couples = (count - 1) // 2
    giver, sink = lengths[1:1 + 2 * couples:2], lengths[2:2 + 2 * couples:2]
    room = jnp.minimum(giver - 1, limit - sink)
    shifted = jax.random.randint(jax.random.fold_in(rng, 1), (couples,), 0, 1 << 20) % (room + 1)
    lengths = lengths.at[1:1 + 2 * couples:2].set(giver - shifted).at[2:2 + 2 * couples:2].set(sink + shifted)
    return lengths[jax.random.permutation(jax.random.fold_in(rng, 2), count)]


def normal_values(stream_key, dims, spread, limit, shards=(), kind=jnp.bfloat16):
    drawn = jax.random.normal(stream_key, dims, jnp.float32) * spread
    if len(shards) > 0:
        drawn = block_scale(stream_key, dims, shards, -0.22, 0.18) * drawn
    return jnp.clip(drawn, min=-limit, max=limit).astype(kind)


def setup_inputs(seed: int = 0) -> dict:
    seeds = jax.random.split(jax.random.key(seed), 8)
    prompt_k = draw_prompt_k(jax.random.fold_in(seeds[7], 71), 0)
    prompt_v = normal_values(seeds[1], (P_SIZE, KVH * HD), 1.0, 6.0, ((0, 128),))
    resp_q = draw_resp_q(jax.random.fold_in(seeds[7], 71), 0)
    resp_k = normal_values(seeds[3], (R, KVH * HD), 1.0, 6.0, ((0, 16), (1, 8)))
    resp_v = normal_values(seeds[4], (R, KVH * HD), 1.0, 6.0, ((0, 16), (1, 8)))
    grad_out = normal_values(seeds[5], (R, H * HD), 1.0, 6.0, ((0, 16), (1, 8)))
    resp_lengths = uneven(seeds[6], NRESP, R, LMAX, 2).astype(jnp.int32)
    return dict(prompt_k=prompt_k, prompt_v=prompt_v, resp_q=resp_q, resp_k=resp_k, resp_v=resp_v, grad_out=grad_out, resp_lengths=resp_lengths)


def segment_of(positions, seg_ends):
    return lax.optimization_barrier(jnp.sum((positions[:, None] >= seg_ends[None, :]).astype(jnp.int32), axis=1))

def head_group(prompt_keys, prompt_values, queries, key_rows, value_rows, cotangent, seg_ends):
    score_scale = 1.0 / math.sqrt(HD)
    q_block = min(512, R)
    window = LMAX + q_block
    padding = jnp.zeros((LMAX, HD), key_rows.dtype)
    padded_keys = jnp.concatenate([padding, key_rows], 0)
    padded_values = jnp.concatenate([padding, value_rows], 0)

    def advance(running, block_index):
        grad_kp, grad_vp, grad_kr, grad_vr = running
        row_start = (block_index * q_block).astype(jnp.int32)
        query_part = lax.dynamic_slice_in_dim(queries, row_start, q_block, 0).astype(jnp.float32)
        cot_part = lax.dynamic_slice_in_dim(cotangent, row_start, q_block, 0).astype(jnp.float32)
        near_keys = lax.dynamic_slice_in_dim(padded_keys, row_start, window, 0)
        near_values = lax.dynamic_slice_in_dim(padded_values, row_start, window, 0)
        row_pos = row_start + jnp.arange(q_block, dtype=jnp.int32)
        key_pos = row_start - LMAX + jnp.arange(window, dtype=jnp.int32)
        allowed = (key_pos[None, :] >= 0) & (key_pos[None, :] <= row_pos[:, None]) & (segment_of(key_pos, seg_ends)[None, :] == segment_of(row_pos, seg_ends)[:, None])
        allowed = jnp.concatenate([jnp.ones((q_block, P_SIZE), dtype=bool), allowed], 1)
        all_keys = jnp.concatenate([prompt_keys, near_keys], 0).astype(jnp.float32)
        all_values = jnp.concatenate([prompt_values, near_values], 0).astype(jnp.float32)
        scores = jnp.einsum('qgd,kd->qgk', query_part, all_keys) * score_scale
        scores = jnp.where(allowed[:, None, :], scores, -jnp.inf)
        row_max = lax.optimization_barrier(jnp.max(scores, axis=-1, keepdims=True))
        log_total = row_max + jnp.log(lax.optimization_barrier(jnp.sum(jnp.exp(scores - row_max), axis=-1, keepdims=True)))
        weights = jnp.exp(scores - log_total)
        rounded = lax.optimization_barrier(weights.astype(jnp.bfloat16)).astype(jnp.float32)
        output = jnp.einsum('qgk,kd->qgd', rounded, all_values).astype(jnp.bfloat16)
        out_wide = lax.optimization_barrier(output).astype(jnp.float32)
        row_delta = lax.optimization_barrier(jnp.sum(cot_part * out_wide, axis=-1, keepdims=True))
        grad_prob = jnp.einsum('qgd,kd->qgk', cot_part, all_values)
        dscore = lax.optimization_barrier((weights * (grad_prob - row_delta) * score_scale).astype(jnp.bfloat16)).astype(jnp.float32)
        grad_query = jnp.einsum('qgk,kd->qgd', dscore, all_keys).astype(jnp.bfloat16)
        grad_key = jnp.einsum('qgk,qgd->kd', dscore, query_part)
        grad_value = jnp.einsum('qgk,qgd->kd', rounded, cot_part)
        grad_kp = grad_kp + grad_key[:P_SIZE]
        grad_vp = grad_vp + grad_value[:P_SIZE]
        grad_kr = lax.dynamic_update_slice_in_dim(grad_kr, lax.dynamic_slice_in_dim(grad_kr, row_start, window, 0) + grad_key[P_SIZE:], row_start, 0)
        grad_vr = lax.dynamic_update_slice_in_dim(grad_vr, lax.dynamic_slice_in_dim(grad_vr, row_start, window, 0) + grad_value[P_SIZE:], row_start, 0)
        return ((grad_kp, grad_vp, grad_kr, grad_vr), (output, grad_query))
    initial = (jnp.zeros((P_SIZE, HD), jnp.float32), jnp.zeros((P_SIZE, HD), jnp.float32), jnp.zeros((R + LMAX, HD), jnp.float32), jnp.zeros((R + LMAX, HD), jnp.float32))
    finals, stacked = lax.scan(advance, initial, jnp.arange(R // q_block, dtype=jnp.int32))
    grad_kp, grad_vp, grad_kr, grad_vr = finals
    group_size = queries.shape[1]
    output = stacked[0].reshape(R, group_size, HD)
    grad_query = stacked[1].reshape(R, group_size, HD)
    return (output, grad_query, grad_kr[LMAX:].astype(jnp.bfloat16), grad_vr[LMAX:].astype(jnp.bfloat16), grad_kp.astype(jnp.bfloat16), grad_vp.astype(jnp.bfloat16))

def reference(prompt_k, prompt_v, resp_q, resp_k, resp_v, grad_out, resp_lengths):
    group_size = H // KVH
    seg_ends = jnp.cumsum(resp_lengths).astype(jnp.int32)
    prompt_keys = prompt_k.reshape(P_SIZE, KVH, HD).transpose(1, 0, 2)
    prompt_values = prompt_v.reshape(P_SIZE, KVH, HD).transpose(1, 0, 2)
    queries = resp_q.reshape(R, KVH, group_size, HD).transpose(1, 0, 2, 3)
    cotangent = grad_out.reshape(R, KVH, group_size, HD).transpose(1, 0, 2, 3)
    key_rows = resp_k.reshape(R, KVH, HD).transpose(1, 0, 2)
    value_rows = resp_v.reshape(R, KVH, HD).transpose(1, 0, 2)

    def per_head(head_items):
        return head_group(head_items[0], head_items[1], head_items[2], head_items[3], head_items[4], head_items[5], seg_ends)
    output, grad_query, grad_kr, grad_vr, grad_kp, grad_vp = lax.map(per_head, (prompt_keys, prompt_values, queries, key_rows, value_rows, cotangent))
    resp_out = output.transpose(1, 0, 2, 3).reshape(R, H * HD)
    grad_q = grad_query.transpose(1, 0, 2, 3).reshape(R, H * HD)
    grad_k_resp = grad_kr.transpose(1, 0, 2).reshape(R, KVH * HD)
    grad_v_resp = grad_vr.transpose(1, 0, 2).reshape(R, KVH * HD)
    grad_k_prompt = grad_kp.transpose(1, 0, 2).reshape(P_SIZE, KVH * HD)
    grad_v_prompt = grad_vp.transpose(1, 0, 2).reshape(P_SIZE, KVH * HD)
    return (resp_out, grad_q, grad_k_resp, grad_v_resp, grad_k_prompt, grad_v_prompt)
```

```python
import functools
import math

import jax
import jax.numpy as jnp
from jax import lax
from jax.experimental import pallas as pl
from jax.experimental.pallas import tpu as pltpu
from jax.sharding import PartitionSpec as P

HD = 128
GROUP = 8
HEADS = 8
ROWS = 256
SPAN = 4
BLOCK = 320
SLAB = 40
CHUNK = 1280
CHUNKS = 5
KEYS = CHUNK * CHUNKS
SCALE = 1.0 / math.sqrt(HD)
EXP2_SCALE = SCALE * math.log2(math.e)
MASKED = -1e30
MESH = pl.DeviceIdType.MESH
F32 = jnp.float32
BF16 = jnp.bfloat16

CHIPS = {1: ((0, 0), (0, 1)), 2: ((0, 3), (0, 2)), 3: ((1, 0), (1, 1)), 4: ((1, 3), (1, 2))}
PLACE = {
    chip: chunk * CHUNK + i * 2 * BLOCK for chunk, two in CHIPS.items() for i, chip in enumerate(two)
}


def dot(a, b):
    return lax.dot_general(a, b, (((1,), (0,)), ((), ())), preferred_element_type=F32)


def key_rows(chunk):
    return pl.ds(pl.multiple_of(chunk * CHUNK, CHUNK), CHUNK)


def kernel(
    lengths,
    prompt_k,
    prompt_v,
    q_hbm,
    resp_k_hbm,
    resp_v_hbm,
    cot_hbm,
    out_ref,
    grad_q_ref,
    grad_k_resp,
    grad_v_resp,
    grad_k_prompt,
    grad_v_prompt,
    q_in,
    cot_in,
    kv,
    k_cols,
    v_cols,
    q_cols,
    q_rows,
    cot_cols,
    cot_scaled,
    cot_rows,
    weights,
    wide_a,
    wide_b,
    mask,
    run_max,
    chunk_max,
    acc,
    delta,
    slab_out,
    slab_in,
    partial,
    from_core,
    from_y,
    from_x,
    to_x,
    from_resp,
    back_out,
    back_in,
    local_sem,
    send_sem,
    recv_sem,
):
    seq = lax.axis_index("seq")
    head = lax.axis_index("head")
    core = seq % 2
    y = (seq // 2) % 4
    x = seq // 8
    first_row = seq * ROWS

    def at(dx, dy, dc):
        return ((((x + dx) % 2) * 4 + (y + dy) % 4) * 2 + (core + dc) % 2, head)

    names = {}

    def link(name, src, dst, device):
        index = names.setdefault(name, len(names))
        return pltpu.make_async_remote_copy(
            src_ref=src,
            dst_ref=dst,
            send_sem=send_sem.at[index],
            recv_sem=recv_sem.at[index],
            device_id=device,
            device_id_type=MESH,
        )

    def slab_link(i):
        return link(("slab", i), slab_out.at[i], slab_in.at[i], (seq, (head + i) % HEADS))

    def resp_link(d):
        return link(
            ("resp", d),
            kv.at[:, pl.ds(SPAN * ROWS, ROWS), :],
            kv.at[:, pl.ds((SPAN - d) * ROWS, ROWS), :],
            ((seq + d) % 16, head),
        )

    def block(chip, dc):
        return kv.at[:, pl.ds(PLACE[chip] + dc * BLOCK, BLOCK), :]

    def y_link(dx, dy):
        return link(("y", dx, dy), block((dx, 0), 0), block((dx, dy), 0), at(0, -dy, 0))

    def x_link():
        return link(("x",), block((0, 0), 0), block((1, 0), 0), at(1, 0, 0))

    def core_link(chip):
        return link(("core", chip), block(chip, 0), block(chip, 1), at(0, 0, 1))

    def core_back(chip):
        row = PLACE[chip] - CHUNK
        return link(
            ("core_back", chip),
            partial.at[:, pl.ds(PLACE[chip] + BLOCK, BLOCK), :],
            from_core.at[:, pl.ds(row // 2, BLOCK), :],
            at(0, 0, 1),
        )

    def y_back(dx, dy):
        return link(
            ("y_back", dx, dy),
            partial.at[:, pl.ds(PLACE[(dx, dy)], BLOCK), :],
            from_y.at[dx, dy - 1],
            at(0, dy, 0),
        )

    def x_back():
        return link(("x_back",), to_x, from_x, at(1, 0, 0))

    def resp_back(d):
        return link(
            ("resp_back", d),
            partial.at[:, pl.ds((SPAN - d) * ROWS, ROWS), :],
            from_resp.at[d - 1],
            ((seq + 16 - d) % 16, head),
        )

    def slab_back(i):
        return link(
            ("slab_back", i), back_out.at[i], back_in.at[i], (seq, (head + HEADS - i) % HEADS)
        )

    loads = [
        pltpu.make_async_copy(
            resp_k_hbm, kv.at[0, pl.ds(SPAN * ROWS, ROWS), :], local_sem.at[0]
        ),
        pltpu.make_async_copy(
            resp_v_hbm, kv.at[1, pl.ds(SPAN * ROWS, ROWS), :], local_sem.at[1]
        ),
        pltpu.make_async_copy(q_hbm, q_in, local_sem.at[2]),
        pltpu.make_async_copy(cot_hbm, cot_in, local_sem.at[3]),
    ]
    for load in loads:
        load.start()
    barrier = pltpu.get_barrier_semaphore()
    for i in range(1, 16):
        pl.semaphore_signal(
            barrier, inc=1, device_id=((seq + i) % 16, head), device_id_type=MESH
        )
    for i in range(1, HEADS):
        pl.semaphore_signal(
            barrier, inc=1, device_id=(seq, (head + i) % HEADS), device_id_type=MESH
        )
    for i in range(HEADS):
        columns = pl.ds(pl.multiple_of(((head + i) % HEADS) * HD, HD), HD)
        slab_out[i, 0] = prompt_k[:, columns].astype(F32)
        slab_out[i, 1] = prompt_v[:, columns].astype(F32)
    pl.semaphore_wait(barrier, 15 + HEADS - 1)
    for i in range(1, HEADS):
        slab_link(i).start()
    loads[0].wait()
    loads[1].wait()
    for d in range(1, SPAN + 1):
        resp_link(d).start()

    loads[2].wait()
    loads[3].wait()
    for g in range(GROUP):
        columns = slice(g * HD, (g + 1) * HD)
        q_rows[g * ROWS : (g + 1) * ROWS, :] = q_in[:, columns]
        q_cols[g] = q_in[:, columns].T
        cot_cols[g] = cot_in[:, columns].astype(F32).T
    token = first_row + lax.broadcasted_iota(jnp.int32, (1, ROWS), 1)
    start = jnp.zeros((1, ROWS), jnp.int32)
    end = jnp.int32(0)
    for i in range(8):
        end = end + lengths[i]
        start = jnp.where(token >= end, end, start)
    key = first_row - SPAN * ROWS + lax.broadcasted_iota(jnp.int32, (CHUNK, ROWS), 0)
    mask[...] = jnp.where((key >= start) & (key <= token), 0.0, MASKED)
    run_max[...] = jnp.full_like(run_max, MASKED)
    acc[...] = jnp.zeros_like(acc)
    cot_scaled[...] = jnp.zeros_like(cot_scaled)
    ones_row = lax.broadcasted_iota(jnp.int32, (16, KEYS), 0) == 0
    v_cols[HD:, :] = jnp.where(ones_row, 1.0, 0.0).astype(BF16)

    for i in range(1, HEADS):
        slab_link(i).wait_recv()
    own = PLACE[(0, 0)]
    for i in range(2):
        slabs = [slab_out[0, i]] + [slab_in[j, i] for j in range(1, HEADS)]
        kv[i, own : own + BLOCK, :] = jnp.concatenate(slabs, axis=0).astype(BF16)
    core_link((0, 0)).start()
    for dy in (1, 3):
        y_link(0, dy).start()
    x_link().start()
    y_link(0, 2).start()

    def turn(chunk):
        rows = key_rows(chunk)
        k_cols[:, rows] = kv[0, rows, :].T
        v_cols[:HD, rows] = kv[1, rows, :].T

    def forward(chunk, masked):
        rows = key_rows(chunk)
        wide = (wide_a, wide_b)

        def scores(g):
            s = dot(kv[0, rows, :], q_cols[g])
            if masked:
                s = s + mask[...]
            wide[g % 2][...] = s
            earlier = run_max[g : g + 1, :]
            largest = jnp.maximum(earlier, jnp.max(s, axis=0, keepdims=True))
            run_max[g : g + 1, :] = largest
            chunk_max[chunk, g : g + 1, :] = largest
            return largest, jnp.exp2((earlier - largest) * EXP2_SCALE)

        def output(g, shrink):
            part = dot(v_cols[:, rows], weights[rows, g * ROWS : (g + 1) * ROWS])
            acc[g] = acc[g] * shrink + part

        largest, shrink = scores(0)
        last = None
        for g in range(GROUP):
            if g + 1 < GROUP:
                following = scores(g + 1)
            w = jnp.exp2((wide[g % 2][...] - largest) * EXP2_SCALE)
            weights[rows, g * ROWS : (g + 1) * ROWS] = w.astype(BF16)
            if last is not None:
                output(g - 1, last)
            last = shrink
            if g + 1 < GROUP:
                largest, shrink = following
        output(GROUP - 1, last)

    for d in range(1, SPAN + 1):
        resp_link(d).wait_recv()
    turn(0)
    forward(0, True)

    def prompt_chunk(chunk, carry):
        @pl.when(chunk == 1)
        def _():
            for dy in (1, 3):
                y_link(0, dy).wait_recv()
                core_link((0, dy)).start()
            core_link((0, 0)).wait_recv()
            core_link((0, 1)).wait_recv()

        @pl.when(chunk == 2)
        def _():
            x_link().wait_recv()
            for dy in (1, 3, 2):
                y_link(1, dy).start()
            core_link((1, 0)).start()
            y_link(0, 2).wait_recv()
            core_link((0, 2)).start()
            core_link((0, 3)).wait_recv()
            core_link((0, 2)).wait_recv()

        @pl.when(chunk == 3)
        def _():
            for dy in (1, 3):
                y_link(1, dy).wait_recv()
                core_link((1, dy)).start()
            core_link((1, 0)).wait_recv()
            core_link((1, 1)).wait_recv()

        @pl.when(chunk == 4)
        def _():
            y_link(1, 2).wait_recv()
            core_link((1, 2)).start()
            core_link((1, 3)).wait_recv()
            core_link((1, 2)).wait_recv()

        turn(chunk)
        forward(chunk, False)
        return carry

    lax.fori_loop(1, CHUNKS, prompt_chunk, 0)

    for g in range(GROUP):
        inverse = 1.0 / acc[g, HD : HD + 1, :]
        rounded = (acc[g, :HD, :] * inverse).astype(BF16)
        out_ref[:, g * HD : (g + 1) * HD] = rounded.T
        delta[g : g + 1, :] = jnp.sum(cot_cols[g] * rounded.astype(F32), axis=0, keepdims=True)
        for chunk in range(CHUNKS):
            chunk_max[chunk, g : g + 1, :] = inverse * jnp.exp2(
                (chunk_max[chunk, g : g + 1, :] - run_max[g : g + 1, :]) * EXP2_SCALE
            )

    is_one = lax.broadcasted_iota(jnp.int32, (CHUNK, HD), 1) < 3
    ones_columns = jnp.where(is_one, 1.0, 0.0).astype(BF16)

    def pair_sum(chip):
        core_back(chip).wait_recv()
        row = PLACE[chip]
        half = (row - CHUNK) // 2
        mine = partial[:, row : row + BLOCK, :].astype(F32)
        partial[:, row : row + BLOCK, :] = (
            mine + from_core[:, half : half + BLOCK, :].astype(F32)
        ).astype(BF16)

    def backward(step, carry):
        chunk = CHUNKS - 1 - step
        rows = key_rows(chunk)
        for g in range(GROUP):
            factor = chunk_max[chunk, g : g + 1, :]
            scaled = (cot_cols[g] * factor).astype(BF16)
            cot_scaled[g, :HD, :] = scaled
            cot_rows[g * ROWS : (g + 1) * ROWS, :] = scaled.T
            rest = -(factor * delta[g : g + 1, :])
            for i in range(3):
                piece = rest.astype(BF16)
                cot_scaled[g, HD + i : HD + i + 1, :] = piece
                rest = rest - piece.astype(F32)
        partial[1, rows, :] = dot(weights[rows, :], cot_rows[...]).astype(BF16)
        values = jnp.concatenate([kv[1, rows, :], ones_columns], axis=1)
        wide = (wide_a, wide_b)
        wide[0][...] = dot(values, cot_scaled[0])
        for g in range(GROUP):
            if g + 1 < GROUP:
                wide[(g + 1) % 2][...] = dot(values, cot_scaled[g + 1])
            columns = slice(g * ROWS, (g + 1) * ROWS)
            weights[rows, columns] = (
                weights[rows, columns].astype(F32) * wide[g % 2][...]
            ).astype(BF16)

        for earlier in (4, 3, 2, 1):

            @pl.when(chunk == earlier - 1)
            def _():
                for chip in CHIPS[earlier]:
                    pair_sum(chip)
                    if chip[1] != 0:
                        y_back(*chip).start()

        partial[0, rows, :] = (dot(weights[rows, :], q_rows[...]) * SCALE).astype(BF16)

        for done in (4, 3, 2, 1):

            @pl.when(chunk == done)
            def _():
                for chip in CHIPS[done]:
                    core_back(chip).start()

        return carry

    lax.fori_loop(0, CHUNKS, backward, 0)

    for d in range(SPAN, 0, -1):
        resp_back(d).start()
    place = PLACE[(1, 0)]
    total = partial[:, place : place + BLOCK, :].astype(F32)
    for dy in (1, 2, 3):
        y_back(1, dy).wait_recv()
        total = total + from_y[1, dy - 1].astype(F32)
    to_x[...] = total.astype(BF16)
    x_back().start()

    def grad_query(g):
        turned = dot(k_cols[...], weights[:, g * ROWS : (g + 1) * ROWS]) * SCALE
        grad_q_ref[:, g * HD : (g + 1) * HD] = turned.astype(BF16).T

    for g in range(GROUP):
        grad_query(g)

    total = partial[:, own : own + BLOCK, :].astype(F32)
    for dy in (1, 2, 3):
        y_back(0, dy).wait_recv()
        total = total + from_y[0, dy - 1].astype(F32)
    x_back().wait_recv()
    total = total + from_x[...].astype(F32)
    for i in range(HEADS):
        back_out[i] = total[:, i * SLAB : (i + 1) * SLAB, :]
    for i in range(1, HEADS):
        slab_back(i).start()

    total = partial[:, SPAN * ROWS : CHUNK, :].astype(F32)
    for d in range(1, SPAN + 1):
        resp_back(d).wait_recv()
        total = total + from_resp[d - 1].astype(F32)
    grad_k_resp[...] = total[0].astype(BF16)
    grad_v_resp[...] = total[1].astype(BF16)

    for i in range(HEADS):
        if i > 0:
            slab_back(i).wait_recv()
        source = back_out if i == 0 else back_in
        columns = pl.ds(pl.multiple_of(((head + i) % HEADS) * HD, HD), HD)
        grad_k_prompt[:, columns] = source[i, 0].astype(BF16)
        grad_v_prompt[:, columns] = source[i, 1].astype(BF16)

    for i in range(1, HEADS):
        slab_link(i).wait_send()
        slab_back(i).wait_send()
    for d in range(1, SPAN + 1):
        resp_link(d).wait_send()
        resp_back(d).wait_send()
    for chip in PLACE:
        core_link(chip).wait_send()
        core_back(chip).wait_send()
        if chip[1] != 0:
            y_link(*chip).wait_send()
            y_back(*chip).wait_send()
    x_link().wait_send()
    x_back().wait_send()


def shards(prompt_k, prompt_v, resp_q, resp_k, resp_v, grad_out, resp_lengths):
    vmem = pl.BlockSpec(memory_space=pltpu.VMEM)
    anywhere = pl.BlockSpec(memory_space=pl.ANY)
    links = 2 * (HEADS - 1) + 2 * SPAN + 2 * (6 + 1 + 8)
    like = jax.ShapeDtypeStruct
    return pl.pallas_call(
        kernel,
        out_shape=(
            like((ROWS, GROUP * HD), BF16),
            like((ROWS, GROUP * HD), BF16),
            like((ROWS, HD), BF16),
            like((ROWS, HD), BF16),
            like((SLAB, HEADS * HD), BF16),
            like((SLAB, HEADS * HD), BF16),
        ),
        in_specs=[pl.BlockSpec(memory_space=pltpu.SMEM), vmem, vmem] + [anywhere] * 4,
        out_specs=[vmem] * 6,
        scratch_shapes=[
            pltpu.VMEM((ROWS, GROUP * HD), BF16),
            pltpu.VMEM((ROWS, GROUP * HD), BF16),
            pltpu.VMEM((2, KEYS, HD), BF16),
            pltpu.VMEM((HD, KEYS), BF16),
            pltpu.VMEM((HD + 16, KEYS), BF16),
            pltpu.VMEM((GROUP, HD, ROWS), BF16),
            pltpu.VMEM((GROUP * ROWS, HD), BF16),
            pltpu.VMEM((GROUP, HD, ROWS), F32),
            pltpu.VMEM((GROUP, 2 * HD, ROWS), BF16),
            pltpu.VMEM((GROUP * ROWS, HD), BF16),
            pltpu.VMEM((KEYS, GROUP * ROWS), BF16),
            pltpu.VMEM((CHUNK, ROWS), F32),
            pltpu.VMEM((CHUNK, ROWS), F32),
            pltpu.VMEM((CHUNK, ROWS), F32),
            pltpu.VMEM((GROUP, ROWS), F32),
            pltpu.VMEM((CHUNKS, GROUP, ROWS), F32),
            pltpu.VMEM((GROUP, HD + 16, ROWS), F32),
            pltpu.VMEM((GROUP, ROWS), F32),
            pltpu.VMEM((HEADS, 2, SLAB, HD), F32),
            pltpu.VMEM((HEADS, 2, SLAB, HD), F32),
            pltpu.VMEM((2, KEYS, HD), BF16),
            pltpu.VMEM((2, 8 * BLOCK, HD), BF16),
            pltpu.VMEM((2, 3, 2, BLOCK, HD), BF16),
            pltpu.VMEM((2, BLOCK, HD), BF16),
            pltpu.VMEM((2, BLOCK, HD), BF16),
            pltpu.VMEM((SPAN, 2, ROWS, HD), BF16),
            pltpu.VMEM((HEADS, 2, SLAB, HD), F32),
            pltpu.VMEM((HEADS, 2, SLAB, HD), F32),
            pltpu.SemaphoreType.DMA((4,)),
            pltpu.SemaphoreType.DMA((links,)),
            pltpu.SemaphoreType.DMA((links,)),
        ],
        compiler_params=pltpu.CompilerParams(
            collective_id=0, has_side_effects=True, vmem_limit_bytes=60 * 2**20
        ),
        cost_estimate=pl.CostEstimate(
            flops=12 * ROWS * GROUP * KEYS * HD,
            bytes_accessed=4 * 2**20,
            transcendentals=ROWS * GROUP * KEYS,
        ),
        name="shared_prompt_attention",
    )(resp_lengths, prompt_k, prompt_v, resp_q, resp_k, resp_v, grad_out)


def solution(mesh):
    placed = (
        P(("seq", "head"), None),
        P(("seq", "head"), None),
        P("seq", "head"),
        P("seq", "head"),
        P("seq", "head"),
        P("seq", "head"),
        P(),
    )
    return jax.shard_map(
        shards,
        mesh=mesh,
        in_specs=placed,
        out_specs=(
            P("seq", "head"),
            P("seq", "head"),
            P("seq", "head"),
            P("seq", "head"),
            P(("seq", "head"), None),
            P(("seq", "head"), None),
        ),
        check_vma=False,
    )
```

```python
import functools
import math

import jax
import jax.numpy as jnp
from jax import lax
from jax.experimental import pallas as pl
from jax.experimental.pallas import tpu as pltpu
from jax.sharding import PartitionSpec as P

HD = 128
GROUP = 8
HEADS = 8
ROWS = 256
SPAN = 4
BLOCK = 320
SLAB = 40
CHUNK = 1280
CHUNKS = 5
KEYS = CHUNK * CHUNKS
SCALE = 1.0 / math.sqrt(HD)
EXP2_SCALE = SCALE * math.log2(math.e)
MASKED = -1e30
MESH = pl.DeviceIdType.MESH
F32 = jnp.float32
BF16 = jnp.bfloat16

CHIPS = {1: ((0, 0), (0, 1)), 2: ((0, 3), (0, 2)), 3: ((1, 0), (1, 1)), 4: ((1, 3), (1, 2))}
PLACE = {
    chip: chunk * CHUNK + i * 2 * BLOCK for chunk, two in CHIPS.items() for i, chip in enumerate(two)
}


def dot(a, b):
    return lax.dot_general(a, b, (((1,), (0,)), ((), ())), preferred_element_type=F32)


def key_rows(chunk):
    return pl.ds(pl.multiple_of(chunk * CHUNK, CHUNK), CHUNK)


def kernel(
    lengths,
    prompt_k,
    prompt_v,
    q_hbm,
    resp_k_hbm,
    resp_v_hbm,
    cot_hbm,
    out_ref,
    grad_q_ref,
    grad_k_resp,
    grad_v_resp,
    grad_k_prompt,
    grad_v_prompt,
    q_in,
    cot_in,
    kv,
    k_cols,
    v_cols,
    q_cols,
    q_rows,
    cot_cols,
    cot_rows,
    weights,
    scaled,
    wide_a,
    wide_b,
    mask,
    run_max,
    chunk_max,
    acc,
    slab_out,
    slab_in,
    partial,
    from_core,
    from_y,
    from_x,
    to_x,
    from_resp,
    from_core_resp,
    back_out,
    back_in,
    local_sem,
    send_sem,
    recv_sem,
):
    seq = lax.axis_index("seq")
    head = lax.axis_index("head")
    core = seq % 2
    y = (seq // 2) % 4
    x = seq // 8
    first_row = seq * ROWS

    def at(dx, dy, dc):
        return ((((x + dx) % 2) * 4 + (y + dy) % 4) * 2 + (core + dc) % 2, head)

    names = {}

    def link(name, src, dst, device):
        index = names.setdefault(name, len(names))
        return pltpu.make_async_remote_copy(
            src_ref=src,
            dst_ref=dst,
            send_sem=send_sem.at[index],
            recv_sem=recv_sem.at[index],
            device_id=device,
            device_id_type=MESH,
        )

    def slab_link(i):
        return link(("slab", i), slab_out.at[i], slab_in.at[i], (seq, (head + i) % HEADS))

    def resp_rows(ref, d):
        return ref.at[:, pl.ds(pl.multiple_of((SPAN - d) * ROWS, ROWS), ROWS), :]

    def resp_link(d):
        return link(
            ("resp", d), resp_rows(kv, 0), resp_rows(kv, d), ((seq + d) % 16, head)
        )

    def core_resp_link(d):
        source = 2 * core + d - 1
        return link(("core_resp", d), resp_rows(kv, source), resp_rows(kv, d), at(0, 0, 1))

    def block(chip, dc):
        return kv.at[:, pl.ds(PLACE[chip] + dc * BLOCK, BLOCK), :]

    def y_link(dx, dy):
        return link(("y", dx, dy), block((dx, 0), 0), block((dx, dy), 0), at(0, -dy, 0))

    def x_link():
        return link(("x",), block((0, 0), 0), block((1, 0), 0), at(1, 0, 0))

    def core_link(chip):
        return link(("core", chip), block(chip, 0), block(chip, 1), at(0, 0, 1))

    def core_back(chip):
        row = PLACE[chip] - CHUNK
        return link(
            ("core_back", chip),
            partial.at[:, pl.ds(PLACE[chip] + BLOCK, BLOCK), :],
            from_core.at[:, pl.ds(row // 2, BLOCK), :],
            at(0, 0, 1),
        )

    def y_back(dx, dy):
        return link(
            ("y_back", dx, dy),
            partial.at[:, pl.ds(PLACE[(dx, dy)], BLOCK), :],
            from_y.at[dx, dy - 1],
            at(0, dy, 0),
        )

    def x_back():
        return link(("x_back",), to_x, from_x, at(1, 0, 0))

    def core_resp_back(d):
        return link(
            ("core_resp_back", d), resp_rows(partial, d), from_core_resp.at[d // 2], at(0, 0, 1)
        )

    def resp_back(d):
        return link(
            ("resp_back", d),
            resp_rows(partial, d),
            from_resp.at[d // 2 - 1],
            ((seq + 16 - d) % 16, head),
        )

    def slab_back(i):
        return link(
            ("slab_back", i), back_out.at[i], back_in.at[i], (seq, (head + HEADS - i) % HEADS)
        )

    loads = [
        pltpu.make_async_copy(
            resp_k_hbm, kv.at[0, pl.ds(SPAN * ROWS, ROWS), :], local_sem.at[0]
        ),
        pltpu.make_async_copy(
            resp_v_hbm, kv.at[1, pl.ds(SPAN * ROWS, ROWS), :], local_sem.at[1]
        ),
        pltpu.make_async_copy(q_hbm, q_in, local_sem.at[2]),
        pltpu.make_async_copy(cot_hbm, cot_in, local_sem.at[3]),
    ]
    for load in loads:
        load.start()
    barrier = pltpu.get_barrier_semaphore()
    partners = [at(0, 0, 1), at(0, 1, 0), at(0, 2, 0), at(0, 3, 0), at(1, 0, 0)]
    partners += [((seq + d) % 16, head) for d in (2, 4, 12, 14)]
    partners += [(seq, (head + i) % HEADS) for i in range(1, HEADS)]
    for partner in partners:
        pl.semaphore_signal(barrier, inc=1, device_id=partner, device_id_type=MESH)
    for i in range(HEADS):
        columns = pl.ds(pl.multiple_of(((head + i) % HEADS) * HD, HD), HD)
        two = (prompt_k[:, columns].astype(F32), prompt_v[:, columns].astype(F32))
        slab_out[i] = jnp.concatenate(two, axis=0).astype(BF16)
    pl.semaphore_wait(barrier, len(partners))
    for i in range(1, HEADS):
        slab_link(i).start()
    loads[0].wait()
    loads[1].wait()
    for d in (4, 2):
        resp_link(d).start()

    loads[2].wait()
    loads[3].wait()
    for g in range(GROUP):
        columns = slice(g * HD, (g + 1) * HD)
        q_rows[g * ROWS : (g + 1) * ROWS, :] = q_in[:, columns]
        q_cols[g] = q_in[:, columns].T
        cot_rows[g * ROWS : (g + 1) * ROWS, :] = cot_in[:, columns]
        cot_cols[g, :HD, :] = cot_in[:, columns].T
        cot_cols[g, HD:, :] = jnp.zeros((HD, ROWS), BF16)
    token = first_row + lax.broadcasted_iota(jnp.int32, (1, ROWS), 1)
    start = jnp.zeros((1, ROWS), jnp.int32)
    end = jnp.int32(0)
    for i in range(8):
        end = end + lengths[i]
        start = jnp.where(token >= end, end, start)
    key = first_row - SPAN * ROWS + lax.broadcasted_iota(jnp.int32, (CHUNK, ROWS), 0)
    mask[...] = jnp.where((key >= start) & (key <= token), 0.0, MASKED)
    run_max[...] = jnp.full_like(run_max, MASKED)
    acc[...] = jnp.zeros_like(acc)
    ones_row = lax.broadcasted_iota(jnp.int32, (16, KEYS), 0) == 0
    v_cols[HD:, :] = jnp.where(ones_row, 1.0, 0.0).astype(BF16)

    for i in range(1, HEADS):
        slab_link(i).wait_recv()
    own = PLACE[(0, 0)]
    slabs = [slab_out[0].astype(F32)] + [slab_in[i].astype(F32) for i in range(1, HEADS)]
    for i in range(2):
        pieces = [slab[i * SLAB : (i + 1) * SLAB, :] for slab in slabs]
        kv[i, own : own + BLOCK, :] = jnp.concatenate(pieces, axis=0).astype(BF16)
    core_link((0, 0)).start()
    for dy in (1, 3):
        y_link(0, dy).start()
    x_link().start()
    y_link(0, 2).start()

    def turn(chunk):
        rows = key_rows(chunk)
        v_cols[:HD, rows] = kv[1, rows, :].T

    def forward(chunk, masked, middle=None):
        rows = key_rows(chunk)
        wide = (wide_a, wide_b)

        def scores(g):
            s = dot(kv[0, rows, :], q_cols[g])
            if masked:
                s = s + mask[...]
            wide[g % 2][...] = s
            earlier = run_max[g : g + 1, :]
            largest = jnp.maximum(earlier, jnp.max(s, axis=0, keepdims=True))
            run_max[g : g + 1, :] = largest
            chunk_max[chunk, g : g + 1, :] = largest
            return largest, jnp.exp2((earlier - largest) * EXP2_SCALE)

        def output(g, shrink):
            part = dot(v_cols[:, rows], weights[rows, g * ROWS : (g + 1) * ROWS])
            acc[g] = acc[g] * shrink + part

        largest, shrink = scores(0)
        last = None
        for g in range(GROUP):
            if g + 1 < GROUP:
                following = scores(g + 1)
            w = jnp.exp2((wide[g % 2][...] - largest) * EXP2_SCALE)
            weights[rows, g * ROWS : (g + 1) * ROWS] = w.astype(BF16)
            if last is not None:
                output(g - 1, last)
            last = shrink
            if middle is not None and g == GROUP // 2:
                middle()
            if g + 1 < GROUP:
                largest, shrink = following
        output(GROUP - 1, last)

    for d in (2, 4):
        resp_link(d).wait_recv()
    for d in (1, 3):
        core_resp_link(d).start()

    def pass_on():
        x_link().wait_recv()
        for dy in (1, 3, 2):
            y_link(1, dy).start()
        core_link((1, 0)).start()
        for dy in (1, 3):
            y_link(0, dy).wait_recv()
            core_link((0, dy)).start()

    for d in (1, 3):
        core_resp_link(d).wait_recv()
    turn(0)
    forward(0, True, pass_on)

    def prompt_chunk(chunk, carry):
        @pl.when(chunk == 1)
        def _():
            y_link(0, 2).wait_recv()
            core_link((0, 2)).start()
            core_link((0, 0)).wait_recv()
            core_link((0, 1)).wait_recv()

        @pl.when(chunk == 2)
        def _():
            for dy in (1, 3):
                y_link(1, dy).wait_recv()
                core_link((1, dy)).start()
            core_link((0, 3)).wait_recv()
            core_link((0, 2)).wait_recv()

        @pl.when(chunk == 3)
        def _():
            y_link(1, 2).wait_recv()
            core_link((1, 2)).start()
            core_link((1, 0)).wait_recv()
            core_link((1, 1)).wait_recv()

        @pl.when(chunk == 4)
        def _():
            core_link((1, 3)).wait_recv()
            core_link((1, 2)).wait_recv()

        turn(chunk)
        forward(chunk, False)
        return carry

    lax.fori_loop(1, CHUNKS, prompt_chunk, 0)

    for g in range(GROUP):
        inverse = 1.0 / acc[g, HD : HD + 1, :]
        rounded = (acc[g, :HD, :] * inverse).astype(BF16)
        out_ref[:, g * HD : (g + 1) * HD] = rounded.T
        products = cot_cols[g, :HD, :].astype(F32) * rounded.astype(F32)
        rest = -jnp.sum(products, axis=0, keepdims=True)
        for i in range(3):
            piece = rest.astype(BF16)
            cot_cols[g, HD + i : HD + i + 1, :] = piece
            rest = rest - piece.astype(F32)
        for chunk in range(CHUNKS):
            chunk_max[chunk, g : g + 1, :] = inverse * jnp.exp2(
                (chunk_max[chunk, g : g + 1, :] - run_max[g : g + 1, :]) * EXP2_SCALE
            )

    is_one = lax.broadcasted_iota(jnp.int32, (CHUNK, HD), 1) < 3
    ones_columns = jnp.where(is_one, 1.0, 0.0).astype(BF16)

    def pair_sum(chip):
        core_back(chip).wait_recv()
        row = PLACE[chip]
        half = (row - CHUNK) // 2
        mine = partial[:, row : row + BLOCK, :].astype(F32)
        partial[:, row : row + BLOCK, :] = (
            mine + from_core[:, half : half + BLOCK, :].astype(F32)
        ).astype(BF16)

    def sum_over_y():
        place = PLACE[(1, 0)]
        total = partial[:, place : place + BLOCK, :].astype(F32)
        for dy in (1, 2, 3):
            y_back(1, dy).wait_recv()
            total = total + from_y[1, dy - 1].astype(F32)
        to_x[...] = total.astype(BF16)
        x_back().start()

    def backward(step, carry):
        chunk = CHUNKS - 1 - step
        rows = key_rows(chunk)
        k_cols[:, rows] = kv[0, rows, :].T
        values = jnp.concatenate([kv[1, rows, :], ones_columns], axis=1)
        wide = (wide_a, wide_b)
        wide[0][...] = dot(values, cot_cols[0])
        for g in range(GROUP):
            if g + 1 < GROUP:
                wide[(g + 1) % 2][...] = dot(values, cot_cols[g + 1])
            columns = slice(g * ROWS, (g + 1) * ROWS)
            w = weights[rows, columns].astype(F32) * chunk_max[chunk, g : g + 1, :]
            scaled[:, columns] = w.astype(BF16)
            weights[rows, columns] = (w * wide[g % 2][...]).astype(BF16)
        for earlier in (4, 3, 2, 1):

            @pl.when(chunk == earlier - 1)
            def _():
                for chip in CHIPS[earlier]:
                    pair_sum(chip)
                    if chip[1] != 0:
                        y_back(*chip).start()

        partial[1, rows, :] = dot(scaled[...], cot_rows[...]).astype(BF16)
        partial[0, rows, :] = (dot(weights[rows, :], q_rows[...]) * SCALE).astype(BF16)

        @pl.when(chunk == 0)
        def _():
            sum_over_y()

        for done in (4, 3, 2, 1):

            @pl.when(chunk == done)
            def _():
                for chip in CHIPS[done]:
                    core_back(chip).start()

        return carry

    lax.fori_loop(0, CHUNKS, backward, 0)

    for d in (1, 3):
        core_resp_back(d).start()

    def grad_query(g):
        turned = dot(k_cols[...], weights[:, g * ROWS : (g + 1) * ROWS]) * SCALE
        grad_q_ref[:, g * HD : (g + 1) * HD] = turned.astype(BF16).T

    for g in range(2):
        grad_query(g)

    for d in (1, 3):
        core_resp_back(d).wait_recv()
        near = pl.ds(pl.multiple_of((SPAN - (2 * core + d - 1)) * ROWS, ROWS), ROWS)
        total = partial[:, near, :].astype(F32) + from_core_resp[d // 2].astype(F32)
        partial[:, near, :] = total.astype(BF16)
    for d in (4, 2):
        resp_back(d).start()

    for g in range(2, 6):
        grad_query(g)

    total = partial[:, own : own + BLOCK, :].astype(F32)
    for dy in (1, 2, 3):
        y_back(0, dy).wait_recv()
        total = total + from_y[0, dy - 1].astype(F32)
    x_back().wait_recv()
    total = total + from_x[...].astype(F32)
    for i in range(HEADS):
        two = [total[j, i * SLAB : (i + 1) * SLAB, :] for j in range(2)]
        back_out[i] = jnp.concatenate(two, axis=0).astype(BF16)
    for i in range(1, HEADS):
        slab_back(i).start()

    for g in range(6, GROUP):
        grad_query(g)

    total = partial[:, SPAN * ROWS : CHUNK, :].astype(F32)
    for d in (2, 4):
        resp_back(d).wait_recv()
        total = total + from_resp[d // 2 - 1].astype(F32)
    grad_k_resp[...] = total[0].astype(BF16)
    grad_v_resp[...] = total[1].astype(BF16)

    for i in range(HEADS):
        if i > 0:
            slab_back(i).wait_recv()
        source = back_out if i == 0 else back_in
        slab = source[i].astype(F32)
        columns = pl.ds(pl.multiple_of(((head + i) % HEADS) * HD, HD), HD)
        grad_k_prompt[:, columns] = slab[:SLAB, :].astype(BF16)
        grad_v_prompt[:, columns] = slab[SLAB:, :].astype(BF16)

    for i in range(1, HEADS):
        slab_link(i).wait_send()
        slab_back(i).wait_send()
    for d in (2, 4):
        resp_link(d).wait_send()
        resp_back(d).wait_send()
    for d in (1, 3):
        core_resp_link(d).wait_send()
        core_resp_back(d).wait_send()
    for chip in PLACE:
        core_link(chip).wait_send()
        core_back(chip).wait_send()
        if chip[1] != 0:
            y_link(*chip).wait_send()
            y_back(*chip).wait_send()
    x_link().wait_send()
    x_back().wait_send()


def write_out(*refs):
    sems = refs[12]
    copies = [pltpu.make_async_copy(refs[i], refs[6 + i], sems.at[i]) for i in range(6)]
    for copy in copies:
        copy.start()
    for copy in copies:
        copy.wait()


def shards(prompt_k, prompt_v, resp_q, resp_k, resp_v, grad_out, resp_lengths):
    vmem = pl.BlockSpec(memory_space=pltpu.VMEM)
    anywhere = pl.BlockSpec(memory_space=pl.ANY)
    links = 2 * (HEADS - 1) + 2 * 4 + 2 * (6 + 1 + 8)
    like = jax.ShapeDtypeStruct
    results = pl.pallas_call(
        kernel,
        out_shape=(
            like((ROWS, GROUP * HD), BF16),
            like((ROWS, GROUP * HD), BF16),
            like((ROWS, HD), BF16),
            like((ROWS, HD), BF16),
            like((SLAB, HEADS * HD), BF16),
            like((SLAB, HEADS * HD), BF16),
        ),
        in_specs=[pl.BlockSpec(memory_space=pltpu.SMEM), vmem, vmem] + [anywhere] * 4,
        out_specs=[vmem] * 6,
        scratch_shapes=[
            pltpu.VMEM((ROWS, GROUP * HD), BF16),
            pltpu.VMEM((ROWS, GROUP * HD), BF16),
            pltpu.VMEM((2, KEYS, HD), BF16),
            pltpu.VMEM((HD, KEYS), BF16),
            pltpu.VMEM((HD + 16, KEYS), BF16),
            pltpu.VMEM((GROUP, HD, ROWS), BF16),
            pltpu.VMEM((GROUP * ROWS, HD), BF16),
            pltpu.VMEM((GROUP, 2 * HD, ROWS), BF16),
            pltpu.VMEM((GROUP * ROWS, HD), BF16),
            pltpu.VMEM((KEYS, GROUP * ROWS), BF16),
            pltpu.VMEM((CHUNK, GROUP * ROWS), BF16),
            pltpu.VMEM((CHUNK, ROWS), F32),
            pltpu.VMEM((CHUNK, ROWS), F32),
            pltpu.VMEM((CHUNK, ROWS), F32),
            pltpu.VMEM((GROUP, ROWS), F32),
            pltpu.VMEM((CHUNKS, GROUP, ROWS), F32),
            pltpu.VMEM((GROUP, HD + 16, ROWS), F32),
            pltpu.VMEM((HEADS, 2 * SLAB, HD), BF16),
            pltpu.VMEM((HEADS, 2 * SLAB, HD), BF16),
            pltpu.VMEM((2, KEYS, HD), BF16),
            pltpu.VMEM((2, 8 * BLOCK, HD), BF16),
            pltpu.VMEM((2, 3, 2, BLOCK, HD), BF16),
            pltpu.VMEM((2, BLOCK, HD), BF16),
            pltpu.VMEM((2, BLOCK, HD), BF16),
            pltpu.VMEM((2, 2, ROWS, HD), BF16),
            pltpu.VMEM((2, 2, ROWS, HD), BF16),
            pltpu.VMEM((HEADS, 2 * SLAB, HD), BF16),
            pltpu.VMEM((HEADS, 2 * SLAB, HD), BF16),
            pltpu.SemaphoreType.DMA((4,)),
            pltpu.SemaphoreType.DMA((links,)),
            pltpu.SemaphoreType.DMA((links,)),
        ],
        compiler_params=pltpu.CompilerParams(
            collective_id=0, has_side_effects=True, vmem_limit_bytes=60 * 2**20
        ),
        cost_estimate=pl.CostEstimate(
            flops=12 * ROWS * GROUP * KEYS * HD,
            bytes_accessed=4 * 2**20,
            transcendentals=ROWS * GROUP * KEYS,
        ),
        name="shared_prompt_attention",
    )(resp_lengths, prompt_k, prompt_v, resp_q, resp_k, resp_v, grad_out)
    return pl.pallas_call(
        write_out,
        out_shape=tuple(like(r.shape, r.dtype) for r in results),
        in_specs=[vmem] * 6,
        out_specs=[anywhere] * 6,
        scratch_shapes=[pltpu.SemaphoreType.DMA((6,))],
        name="write_out",
    )(*results)


def solution(mesh):
    placed = (
        P(("seq", "head"), None),
        P(("seq", "head"), None),
        P("seq", "head"),
        P("seq", "head"),
        P("seq", "head"),
        P("seq", "head"),
        P(),
    )
    return jax.shard_map(
        shards,
        mesh=mesh,
        in_specs=placed,
        out_specs=(
            P("seq", "head"),
            P("seq", "head"),
            P("seq", "head"),
            P("seq", "head"),
            P(("seq", "head"), None),
            P(("seq", "head"), None),
        ),
        check_vma=False,
    )
```

```python
import functools
import math

import jax
import jax.numpy as jnp
from jax import lax
from jax.experimental import pallas as pl
from jax.experimental.pallas import tpu as pltpu
from jax.sharding import PartitionSpec as P

HD = 128
GROUP = 8
HEADS = 8
ROWS = 256
SPAN = 4
BLOCK = 320
SLAB = 40
WIDE = 4
CHUNK = 1280
CHUNKS = 5
KEYS = CHUNK * CHUNKS
SCALE = 1.0 / math.sqrt(HD)
EXP2_SCALE = SCALE * math.log2(math.e)
MASKED = -1e30
MESH = pl.DeviceIdType.MESH
F32 = jnp.float32
BF16 = jnp.bfloat16

CHIPS = {1: ((0, 0), (0, 1)), 2: ((0, 3), (0, 2)), 3: ((1, 0), (1, 1)), 4: ((1, 3), (1, 2))}
PLACE = {
    chip: chunk * CHUNK + i * 2 * BLOCK for chunk, two in CHIPS.items() for i, chip in enumerate(two)
}


def dot(a, b):
    return lax.dot_general(a, b, (((1,), (0,)), ((), ())), preferred_element_type=F32)


def key_rows(chunk):
    return pl.ds(pl.multiple_of(chunk * CHUNK, CHUNK), CHUNK)


def kernel(
    lengths,
    prompt_k,
    prompt_v,
    q_hbm,
    resp_k_hbm,
    resp_v_hbm,
    cot_hbm,
    out_ref,
    grad_q_ref,
    grad_k_resp,
    grad_v_resp,
    grad_k_prompt,
    grad_v_prompt,
    kv,
    k_cols,
    v_cols,
    q_cols,
    q_rows,
    cot_cols,
    cot_rows,
    weights,
    scaled,
    wide,
    run_max,
    chunk_max,
    acc,
    slab_out,
    slab_in,
    partial,
    from_core,
    from_y,
    from_x,
    from_resp,
    from_core_resp,
    back_out,
    back_in,
    local_sem,
    send_sem,
    recv_sem,
):
    seq = lax.axis_index("seq")
    head = lax.axis_index("head")
    core = seq % 2
    y = (seq // 2) % 4
    x = seq // 8
    first_row = seq * ROWS

    def at(dx, dy, dc):
        return ((((x + dx) % 2) * 4 + (y + dy) % 4) * 2 + (core + dc) % 2, head)

    names = {}

    def link(name, src, dst, device):
        index = names.setdefault(name, len(names))
        return pltpu.make_async_remote_copy(
            src_ref=src,
            dst_ref=dst,
            send_sem=send_sem.at[index],
            recv_sem=recv_sem.at[index],
            device_id=device,
            device_id_type=MESH,
        )

    def slab_link(i):
        return link(("slab", i), slab_out.at[i], slab_in.at[i], (seq, (head + i) % HEADS))

    def resp_rows(ref, d):
        return ref.at[:, pl.ds(pl.multiple_of((SPAN - d) * ROWS, ROWS), ROWS), :]

    def resp_link(d):
        return link(
            ("resp", d), resp_rows(kv, 0), resp_rows(kv, d), ((seq + d) % 16, head)
        )

    def core_resp_link(d):
        source = 2 * core + d - 1
        return link(("core_resp", d), resp_rows(kv, source), resp_rows(kv, d), at(0, 0, 1))

    def block(chip, dc):
        return kv.at[:, pl.ds(PLACE[chip] + dc * BLOCK, BLOCK), :]

    def y_link(dx, dy):
        return link(("y", dx, dy), block((dx, 0), 0), block((dx, dy), 0), at(0, -dy, 0))

    def x_link():
        return link(("x",), block((0, 0), 0), block((1, 0), 0), at(1, 0, 0))

    def core_link(chip):
        return link(("core", chip), block(chip, 0), block(chip, 1), at(0, 0, 1))

    def core_back(chip):
        row = PLACE[chip] - CHUNK
        return link(
            ("core_back", chip),
            partial.at[:, pl.ds(PLACE[chip] + BLOCK, BLOCK), :],
            from_core.at[:, pl.ds(row // 2, BLOCK), :],
            at(0, 0, 1),
        )

    def y_back(dx, dy):
        return link(
            ("y_back", dx, dy),
            partial.at[:, pl.ds(PLACE[(dx, dy)], BLOCK), :],
            from_y.at[dx, dy - 1],
            at(0, dy, 0),
        )

    def x_back():
        sums = partial.at[:, pl.ds(PLACE[(1, 0)], BLOCK), :]
        return link(("x_back",), sums, from_x, at(1, 0, 0))

    def core_resp_back(d):
        return link(
            ("core_resp_back", d), resp_rows(partial, d), from_core_resp.at[d // 2], at(0, 0, 1)
        )

    def resp_back(d):
        return link(
            ("resp_back", d),
            resp_rows(partial, d),
            from_resp.at[d // 2 - 1],
            ((seq + 16 - d) % 16, head),
        )

    def slab_back(i):
        return link(
            ("slab_back", i), back_out.at[i], back_in.at[i], (seq, (head + HEADS - i) % HEADS)
        )

    loads = [
        pltpu.make_async_copy(
            resp_k_hbm, kv.at[0, pl.ds(SPAN * ROWS, ROWS), :], local_sem.at[0]
        ),
        pltpu.make_async_copy(
            resp_v_hbm, kv.at[1, pl.ds(SPAN * ROWS, ROWS), :], local_sem.at[1]
        ),
    ]
    for g in range(GROUP):
        columns, rows = pl.ds(g * HD, HD), pl.ds(g * ROWS, ROWS)
        for i, (array, by_head) in enumerate(((q_hbm, q_rows), (cot_hbm, cot_rows))):
            loads.append(
                pltpu.make_async_copy(
                    array.at[:, columns], by_head.at[rows, :], local_sem.at[2 + 2 * g + i]
                )
            )
    for load in loads:
        load.start()
    barrier = pltpu.get_barrier_semaphore()
    partners = [at(0, 0, 1), at(0, 1, 0), at(0, 2, 0), at(0, 3, 0), at(1, 0, 0)]
    partners += [((seq + d) % 16, head) for d in (2, 4, 12, 14)]
    partners += [(seq, (head + i) % HEADS) for i in range(1, HEADS)]
    for partner in partners:
        pl.semaphore_signal(barrier, inc=1, device_id=partner, device_id_type=MESH)
    for i in range(HEADS):
        columns = pl.ds(pl.multiple_of(((head + i) % HEADS) * HD, HD), HD)
        two = (prompt_k[:, columns].astype(F32), prompt_v[:, columns].astype(F32))
        slab_out[i] = jnp.concatenate(two, axis=0).astype(BF16)
    pl.semaphore_wait(barrier, len(partners))
    for i in range(1, HEADS):
        slab_link(i).start()

    loads[0].wait()
    loads[1].wait()
    for d in (4, 2):

        @pl.when(seq + d < 16)
        def _():
            resp_link(d).start()

    for load in loads[2:]:
        load.wait()
    for g in range(GROUP):
        rows = slice(g * ROWS, (g + 1) * ROWS)
        q_cols[g] = q_rows[rows, :].T
        cot_cols[g, :HD, :] = cot_rows[rows, :].T
        cot_cols[g, HD:, :] = jnp.zeros((HD, ROWS), BF16)
    token = first_row + lax.broadcasted_iota(jnp.int32, (1, ROWS), 1)
    start = jnp.zeros((1, ROWS), jnp.int32)
    end = jnp.int32(0)
    for i in range(8):
        end = end + lengths[i]
        start = jnp.where(token >= end, end, start)
    key = first_row - SPAN * ROWS + lax.broadcasted_iota(jnp.int32, (CHUNK, ROWS), 0)
    allowed = (key >= start) & (key <= token)
    scaled[:, :ROWS] = jnp.where(allowed, 0.0, MASKED).astype(BF16)
    run_max[...] = jnp.full_like(run_max, MASKED)
    acc[...] = jnp.zeros_like(acc)
    ones_row = lax.broadcasted_iota(jnp.int32, (16, CHUNK), 0) == 0
    v_cols[HD:, :] = jnp.where(ones_row, 1.0, 0.0).astype(BF16)

    for i in range(1, HEADS):
        slab_link(i).wait_recv()
    own = PLACE[(0, 0)]
    slabs = [slab_out[0].astype(F32)] + [slab_in[i].astype(F32) for i in range(1, HEADS)]
    for i in range(2):
        pieces = [slab[i * SLAB : (i + 1) * SLAB, :] for slab in slabs]
        kv[i, own : own + BLOCK, :] = jnp.concatenate(pieces, axis=0).astype(BF16)
    core_link((0, 0)).start()
    for dy in (1, 3):
        y_link(0, dy).start()
    x_link().start()
    y_link(0, 2).start()

    def turn(chunk):
        rows = key_rows(chunk)
        v_cols[:HD, :] = kv[1, rows, :].T

    def forward(chunk, masked, middle):
        rows = key_rows(chunk)

        def scores(g):
            s = dot(kv[0, rows, :], q_cols[g])
            if masked:
                s = s + scaled[:, :ROWS].astype(F32)
            wide[g % WIDE] = s
            earlier = run_max[g : g + 1, :]
            largest = jnp.maximum(earlier, jnp.max(s, axis=0, keepdims=True))
            run_max[g : g + 1, :] = largest
            chunk_max[chunk, g : g + 1, :] = largest
            return jnp.exp2((earlier - largest) * EXP2_SCALE)

        def output(g, shrink):
            columns = slice(g * ROWS, (g + 1) * ROWS)
            largest = chunk_max[chunk, g : g + 1, :]
            w = jnp.exp2((wide[g % WIDE] - largest) * EXP2_SCALE).astype(BF16)
            weights[rows, columns] = w
            acc[g] = acc[g] * shrink + dot(v_cols[...], weights[rows, columns])

        for first in range(0, GROUP, WIDE):
            some = range(first, first + WIDE)
            shrinks = [scores(g) for g in some]
            middle(first // WIDE)

            @pl.when(seq >= 0)
            def _():
                for g, shrink in zip(some, shrinks):
                    output(g, shrink)

    def during_near(half):
        if half == 0:
            y_link(0, 3).wait_recv()
            core_link((0, 3)).start()
            core_link((1, 0)).start()
        else:
            y_link(0, 2).wait_recv()
            core_link((0, 2)).start()

    def during_far(half):
        if half == 1:
            for d in (2, 4):

                @pl.when(seq >= d)
                def _():
                    resp_link(d).wait_recv()

                @pl.when(seq < d)
                def _():
                    first = (SPAN - d) * ROWS
                    kv[:, first : first + ROWS, :] = jnp.zeros((2, ROWS, HD), BF16)

            for d in (1, 3):
                core_resp_link(d).start()

    def during_resp(half):
        if half == 0:
            for dy in (1, 3):
                y_link(1, dy).wait_recv()
                core_link((1, dy)).start()

    y_link(0, 1).wait_recv()
    core_link((0, 1)).start()
    x_link().wait_recv()
    for dy in (1, 3, 2):
        y_link(1, dy).start()
    core_link((0, 0)).wait_recv()
    core_link((0, 1)).wait_recv()
    turn(1)
    forward(1, False, during_near)

    core_link((0, 3)).wait_recv()
    core_link((0, 2)).wait_recv()
    turn(2)
    forward(2, False, during_far)

    for d in (1, 3):
        core_resp_link(d).wait_recv()
    turn(0)
    forward(0, True, during_resp)

    def prompt_chunk(chunk, carry):
        @pl.when(chunk == 3)
        def _():
            core_link((1, 0)).wait_recv()
            core_link((1, 1)).wait_recv()

        @pl.when(chunk == 4)
        def _():
            core_link((1, 3)).wait_recv()
            core_link((1, 2)).wait_recv()

        def during(half):
            if half == 0:

                @pl.when(chunk == 3)
                def _():
                    y_link(1, 2).wait_recv()
                    core_link((1, 2)).start()

        turn(chunk)
        forward(chunk, False, during)
        return carry

    lax.fori_loop(3, CHUNKS, prompt_chunk, 0)

    for g in range(GROUP):
        inverse = 1.0 / acc[g, HD : HD + 1, :]
        rounded = (acc[g, :HD, :] * inverse).astype(BF16)
        scaled[:ROWS, g * HD : (g + 1) * HD] = rounded.T
        products = cot_cols[g, :HD, :].astype(F32) * rounded.astype(F32)
        rest = -jnp.sum(products, axis=0, keepdims=True)
        for i in range(3):
            piece = rest.astype(BF16)
            cot_cols[g, HD + i : HD + i + 1, :] = piece
            rest = rest - piece.astype(F32)
        for chunk in range(CHUNKS):
            chunk_max[chunk, g : g + 1, :] = inverse * jnp.exp2(
                (chunk_max[chunk, g : g + 1, :] - run_max[g : g + 1, :]) * EXP2_SCALE
            )

    out_copy = pltpu.make_async_copy(
        scaled.at[pl.ds(0, ROWS), pl.ds(0, GROUP * HD)], out_ref, local_sem.at[2 + 2 * GROUP]
    )
    out_copy.start()
    is_one = lax.broadcasted_iota(jnp.int32, (CHUNK, HD), 1) < 3
    ones_columns = jnp.where(is_one, 1.0, 0.0).astype(BF16)

    def pair_sum(chip):
        core_back(chip).wait_recv()
        row = PLACE[chip]
        half = (row - CHUNK) // 2
        mine = partial[:, row : row + BLOCK, :].astype(F32)
        partial[:, row : row + BLOCK, :] = (
            mine + from_core[:, half : half + BLOCK, :].astype(F32)
        ).astype(BF16)

    def sum_over_y():
        place = PLACE[(1, 0)]
        total = partial[:, place : place + BLOCK, :].astype(F32)
        for dy in (1, 2, 3):
            y_back(1, dy).wait_recv()
            total = total + from_y[1, dy - 1].astype(F32)
        partial[:, place : place + BLOCK, :] = total.astype(BF16)
        x_back().start()

    def backward(chunk, middle=None):
        rows = key_rows(chunk)
        k_cols[:, rows] = kv[0, rows, :].T
        values = jnp.concatenate([kv[1, rows, :], ones_columns], axis=1)
        for g in range(GROUP):
            columns = slice(g * ROWS, (g + 1) * ROWS)
            wide[g % WIDE] = dot(values, cot_cols[g])
            w = weights[rows, columns].astype(F32) * chunk_max[chunk, g : g + 1, :]
            scaled[:, columns] = w.astype(BF16)
            weights[rows, columns] = (w * wide[g % WIDE]).astype(BF16)
        if middle is not None:
            middle()
        partial[1, rows, :] = dot(scaled[...], cot_rows[...]).astype(BF16)
        partial[0, rows, :] = (dot(weights[rows, :], q_rows[...]) * SCALE).astype(BF16)

    def pass_back(chunk):
        for chip in CHIPS[chunk]:
            pair_sum(chip)
            if chip[1] != 0:
                y_back(*chip).start()

    def prompt_back(step, carry):
        chunk = CHUNKS - 1 - step
        for later in (1, 2):

            @pl.when(chunk == later)
            def _():
                pass_back(later + 2)

        backward(chunk)
        for done in (4, 3, 2, 1):

            @pl.when(chunk == done)
            def _():
                for chip in CHIPS[done]:
                    core_back(chip).start()

        return carry

    out_copy.wait()
    lax.fori_loop(0, CHUNKS - 1, prompt_back, 0)
    pass_back(2)

    def last_sums():
        @pl.when(seq >= 0)
        def _():
            pass_back(1)
            sum_over_y()

    backward(0, last_sums)

    for d in (1, 3):
        core_resp_back(d).start()

    def grad_query(g):
        turned = dot(k_cols[...], weights[:, g * ROWS : (g + 1) * ROWS]) * SCALE
        grad_q_ref[:, g * HD : (g + 1) * HD] = turned.astype(BF16).T

    for g in range(2):
        grad_query(g)

    for d in (1, 3):
        core_resp_back(d).wait_recv()
        near = pl.ds(pl.multiple_of((SPAN - (2 * core + d - 1)) * ROWS, ROWS), ROWS)
        total = partial[:, near, :].astype(F32) + from_core_resp[d // 2].astype(F32)
        partial[:, near, :] = total.astype(BF16)
    for d in (4, 2):

        @pl.when(seq >= d)
        def _():
            resp_back(d).start()

    for g in range(2, 6):
        grad_query(g)

    total = partial[:, own : own + BLOCK, :].astype(F32)
    for dy in (1, 2, 3):
        y_back(0, dy).wait_recv()
        total = total + from_y[0, dy - 1].astype(F32)
    x_back().wait_recv()
    total = total + from_x[...].astype(F32)
    for i in range(HEADS):
        two = [total[j, i * SLAB : (i + 1) * SLAB, :] for j in range(2)]
        back_out[i] = jnp.concatenate(two, axis=0).astype(BF16)
    for i in range(1, HEADS):
        slab_back(i).start()

    for g in range(6, GROUP):
        grad_query(g)

    total = partial[:, SPAN * ROWS : CHUNK, :].astype(F32)
    for d in (2, 4):

        @pl.when(seq + d < 16)
        def _():
            resp_back(d).wait_recv()

        @pl.when(seq + d >= 16)
        def _():
            from_resp[d // 2 - 1] = jnp.zeros((2, ROWS, HD), BF16)

        total = total + from_resp[d // 2 - 1].astype(F32)
    grad_k_resp[...] = total[0].astype(BF16)
    grad_v_resp[...] = total[1].astype(BF16)

    for i in range(HEADS):
        if i > 0:
            slab_back(i).wait_recv()
        source = back_out if i == 0 else back_in
        slab = source[i].astype(F32)
        columns = pl.ds(pl.multiple_of(((head + i) % HEADS) * HD, HD), HD)
        grad_k_prompt[:, columns] = slab[:SLAB, :].astype(BF16)
        grad_v_prompt[:, columns] = slab[SLAB:, :].astype(BF16)

    for i in range(1, HEADS):
        slab_link(i).wait_send()
        slab_back(i).wait_send()
    for d in (2, 4):

        @pl.when(seq + d < 16)
        def _():
            resp_link(d).wait_send()

        @pl.when(seq >= d)
        def _():
            resp_back(d).wait_send()

    for d in (1, 3):
        core_resp_link(d).wait_send()
        core_resp_back(d).wait_send()
    for chip in PLACE:
        core_link(chip).wait_send()
        core_back(chip).wait_send()
        if chip[1] != 0:
            y_link(*chip).wait_send()
            y_back(*chip).wait_send()
    x_link().wait_send()
    x_back().wait_send()


def write_out(*refs):
    sems = refs[12]
    copies = [pltpu.make_async_copy(refs[i], refs[6 + i], sems.at[i]) for i in range(6)]
    for copy in copies:
        copy.start()
    for copy in copies:
        copy.wait()


def shards(prompt_k, prompt_v, resp_q, resp_k, resp_v, grad_out, resp_lengths):
    vmem = pl.BlockSpec(memory_space=pltpu.VMEM)
    anywhere = pl.BlockSpec(memory_space=pl.ANY)
    links = 2 * (HEADS - 1) + 2 * 4 + 2 * (6 + 1 + 8)
    like = jax.ShapeDtypeStruct
    results = pl.pallas_call(
        kernel,
        out_shape=(
            like((ROWS, GROUP * HD), BF16),
            like((ROWS, GROUP * HD), BF16),
            like((ROWS, HD), BF16),
            like((ROWS, HD), BF16),
            like((SLAB, HEADS * HD), BF16),
            like((SLAB, HEADS * HD), BF16),
        ),
        in_specs=[pl.BlockSpec(memory_space=pltpu.SMEM), vmem, vmem] + [anywhere] * 4,
        out_specs=[anywhere] + [vmem] * 5,
        scratch_shapes=[
            pltpu.VMEM((2, KEYS, HD), BF16),
            pltpu.VMEM((HD, KEYS), BF16),
            pltpu.VMEM((HD + 16, CHUNK), BF16),
            pltpu.VMEM((GROUP, HD, ROWS), BF16),
            pltpu.VMEM((GROUP * ROWS, HD), BF16),
            pltpu.VMEM((GROUP, 2 * HD, ROWS), BF16),
            pltpu.VMEM((GROUP * ROWS, HD), BF16),
            pltpu.VMEM((KEYS, GROUP * ROWS), BF16),
            pltpu.VMEM((CHUNK, GROUP * ROWS), BF16),
            pltpu.VMEM((WIDE, CHUNK, ROWS), F32),
            pltpu.VMEM((GROUP, ROWS), F32),
            pltpu.VMEM((CHUNKS, GROUP, ROWS), F32),
            pltpu.VMEM((GROUP, HD + 16, ROWS), F32),
            pltpu.VMEM((HEADS, 2 * SLAB, HD), BF16),
            pltpu.VMEM((HEADS, 2 * SLAB, HD), BF16),
            pltpu.VMEM((2, KEYS, HD), BF16),
            pltpu.VMEM((2, 8 * BLOCK, HD), BF16),
            pltpu.VMEM((2, 3, 2, BLOCK, HD), BF16),
            pltpu.VMEM((2, BLOCK, HD), BF16),
            pltpu.VMEM((2, 2, ROWS, HD), BF16),
            pltpu.VMEM((2, 2, ROWS, HD), BF16),
            pltpu.VMEM((HEADS, 2 * SLAB, HD), BF16),
            pltpu.VMEM((HEADS, 2 * SLAB, HD), BF16),
            pltpu.SemaphoreType.DMA((3 + 2 * GROUP,)),
            pltpu.SemaphoreType.DMA((links,)),
            pltpu.SemaphoreType.DMA((links,)),
        ],
        compiler_params=pltpu.CompilerParams(
            collective_id=0, has_side_effects=True, vmem_limit_bytes=63 * 2**20
        ),
        cost_estimate=pl.CostEstimate(
            flops=12 * ROWS * GROUP * KEYS * HD,
            bytes_accessed=4 * 2**20,
            transcendentals=ROWS * GROUP * KEYS,
        ),
        name="shared_prompt_attention",
    )(resp_lengths, prompt_k, prompt_v, resp_q, resp_k, resp_v, grad_out)
    return pl.pallas_call(
        write_out,
        out_shape=tuple(like(r.shape, r.dtype) for r in results),
        in_specs=[vmem] * 6,
        out_specs=[anywhere] * 6,
        scratch_shapes=[pltpu.SemaphoreType.DMA((6,))],
        name="write_out",
    )(*results)


def solution(mesh):
    placed = (
        P(("seq", "head"), None),
        P(("seq", "head"), None),
        P("seq", "head"),
        P("seq", "head"),
        P("seq", "head"),
        P("seq", "head"),
        P(),
    )
    return jax.shard_map(
        shards,
        mesh=mesh,
        in_specs=placed,
        out_specs=(
            P("seq", "head"),
            P("seq", "head"),
            P("seq", "head"),
            P("seq", "head"),
            P(("seq", "head"), None),
            P(("seq", "head"), None),
        ),
        check_vma=False,
    )
```

```python
import functools
import math

import jax
import jax.numpy as jnp
from jax import lax
from jax.experimental import pallas as pl
from jax.experimental.pallas import tpu as pltpu
from jax.sharding import PartitionSpec as P

HD = 128
GROUP = 8
HEADS = 8
ROWS = 256
SPAN = 4
BLOCK = 320
SLAB = 40
WIDE = 4
CHUNK = 1280
CHUNKS = 5
KEYS = CHUNK * CHUNKS
SCALE = 1.0 / math.sqrt(HD)
EXP2_SCALE = SCALE * math.log2(math.e)
MASKED = -1e30
MESH = pl.DeviceIdType.MESH
F32 = jnp.float32
BF16 = jnp.bfloat16

CHIPS = {1: ((0, 0), (0, 1)), 2: ((0, 3), (0, 2)), 3: ((1, 0), (1, 1)), 4: ((1, 3), (1, 2))}
PLACE = {
    chip: chunk * CHUNK + i * 2 * BLOCK for chunk, two in CHIPS.items() for i, chip in enumerate(two)
}


def dot(a, b):
    return lax.dot_general(a, b, (((1,), (0,)), ((), ())), preferred_element_type=F32)


def key_rows(chunk):
    return pl.ds(pl.multiple_of(chunk * CHUNK, CHUNK), CHUNK)


def kernel(
    lengths,
    prompt_k,
    prompt_v,
    q_hbm,
    resp_k_hbm,
    resp_v_hbm,
    cot_hbm,
    out_ref,
    grad_q_ref,
    grad_k_resp,
    grad_v_resp,
    grad_k_prompt,
    grad_v_prompt,
    kv,
    k_cols,
    v_cols,
    q_cols,
    q_rows,
    cot_cols,
    cot_rows,
    weights,
    scaled,
    wide,
    run_max,
    chunk_max,
    acc,
    slab_out,
    slab_in,
    partial,
    from_core,
    from_y,
    from_x,
    from_resp,
    from_core_resp,
    back_out,
    back_in,
    local_sem,
    send_sem,
    recv_sem,
):
    seq = lax.axis_index("seq")
    head = lax.axis_index("head")
    core = seq % 2
    y = (seq // 2) % 4
    x = seq // 8
    first_row = seq * ROWS

    def at(dx, dy, dc):
        return ((((x + dx) % 2) * 4 + (y + dy) % 4) * 2 + (core + dc) % 2, head)

    names = {}

    def link(name, src, dst, device):
        index = names.setdefault(name, len(names))
        return pltpu.make_async_remote_copy(
            src_ref=src,
            dst_ref=dst,
            send_sem=send_sem.at[index],
            recv_sem=recv_sem.at[index],
            device_id=device,
            device_id_type=MESH,
        )

    def slab_link(i):
        return link(("slab", i), slab_out.at[i], slab_in.at[i], (seq, (head + i) % HEADS))

    def resp_rows(ref, d):
        return ref.at[:, pl.ds(pl.multiple_of((SPAN - d) * ROWS, ROWS), ROWS), :]

    def resp_link(d):
        return link(
            ("resp", d), resp_rows(kv, 0), resp_rows(kv, d), ((seq + d) % 16, head)
        )

    def core_resp_link(d):
        source = 2 * core + d - 1
        return link(("core_resp", d), resp_rows(kv, source), resp_rows(kv, d), at(0, 0, 1))

    def block(chip, dc):
        return kv.at[:, pl.ds(PLACE[chip] + dc * BLOCK, BLOCK), :]

    def y_link(dx, dy):
        return link(("y", dx, dy), block((dx, 0), 0), block((dx, dy), 0), at(0, -dy, 0))

    def x_link():
        return link(("x",), block((0, 0), 0), block((1, 0), 0), at(1, 0, 0))

    def core_link(chip):
        return link(("core", chip), block(chip, 0), block(chip, 1), at(0, 0, 1))

    def core_back(chip):
        row = PLACE[chip] - CHUNK
        return link(
            ("core_back", chip),
            partial.at[:, pl.ds(PLACE[chip] + BLOCK, BLOCK), :],
            from_core.at[:, pl.ds(row // 2, BLOCK), :],
            at(0, 0, 1),
        )

    def y_back(dx, dy):
        return link(
            ("y_back", dx, dy),
            partial.at[:, pl.ds(PLACE[(dx, dy)], BLOCK), :],
            from_y.at[dx, dy - 1],
            at(0, dy, 0),
        )

    def x_back():
        sums = partial.at[:, pl.ds(PLACE[(1, 0)], BLOCK), :]
        return link(("x_back",), sums, from_x, at(1, 0, 0))

    def core_resp_back(d):
        return link(
            ("core_resp_back", d), resp_rows(partial, d), from_core_resp.at[d // 2], at(0, 0, 1)
        )

    def resp_back(d):
        return link(
            ("resp_back", d),
            resp_rows(partial, d),
            from_resp.at[d // 2 - 1],
            ((seq + 16 - d) % 16, head),
        )

    def slab_back(i):
        return link(
            ("slab_back", i), back_out.at[i], back_in.at[i], (seq, (head + HEADS - i) % HEADS)
        )

    loads = [
        pltpu.make_async_copy(
            resp_k_hbm, kv.at[0, pl.ds(SPAN * ROWS, ROWS), :], local_sem.at[0]
        ),
        pltpu.make_async_copy(
            resp_v_hbm, kv.at[1, pl.ds(SPAN * ROWS, ROWS), :], local_sem.at[1]
        ),
    ]
    for g in range(GROUP):
        columns, rows = pl.ds(g * HD, HD), pl.ds(g * ROWS, ROWS)
        for i, (array, by_head) in enumerate(((q_hbm, q_rows), (cot_hbm, cot_rows))):
            loads.append(
                pltpu.make_async_copy(
                    array.at[:, columns], by_head.at[rows, :], local_sem.at[2 + 2 * g + i]
                )
            )
    for load in loads:
        load.start()
    barrier = pltpu.get_barrier_semaphore()
    partners = [at(0, 0, 1), at(0, 1, 0), at(0, 2, 0), at(0, 3, 0), at(1, 0, 0)]
    partners += [((seq + d) % 16, head) for d in (2, 4, 12, 14)]
    partners += [(seq, (head + i) % HEADS) for i in range(1, HEADS)]
    for partner in partners:
        pl.semaphore_signal(barrier, inc=1, device_id=partner, device_id_type=MESH)
    for i in range(HEADS):
        columns = pl.ds(pl.multiple_of(((head + i) % HEADS) * HD, HD), HD)
        two = (prompt_k[:, columns].astype(F32), prompt_v[:, columns].astype(F32))
        slab_out[i] = jnp.concatenate(two, axis=0).astype(BF16)
    pl.semaphore_wait(barrier, len(partners))
    for i in range(1, HEADS):
        slab_link(i).start()

    loads[0].wait()
    loads[1].wait()
    for d in (4, 2):

        @pl.when(seq + d < 16)
        def _():
            resp_link(d).start()

    for load in loads[2:]:
        load.wait()
    for g in range(GROUP):
        rows = slice(g * ROWS, (g + 1) * ROWS)
        q_cols[g] = q_rows[rows, :].T
        cot_cols[g, :HD, :] = cot_rows[rows, :].T
        cot_cols[g, HD:, :] = jnp.zeros((HD, ROWS), BF16)
    token = first_row + lax.broadcasted_iota(jnp.int32, (1, ROWS), 1)
    start = jnp.zeros((1, ROWS), jnp.int32)
    end = jnp.int32(0)
    for i in range(8):
        end = end + lengths[i]
        start = jnp.where(token >= end, end, start)
    key = first_row - SPAN * ROWS + lax.broadcasted_iota(jnp.int32, (CHUNK, ROWS), 0)
    allowed = (key >= start) & (key <= token)
    scaled[:, :ROWS] = jnp.where(allowed, 0.0, MASKED).astype(BF16)
    run_max[...] = jnp.full_like(run_max, MASKED)
    acc[...] = jnp.zeros_like(acc)
    ones_row = lax.broadcasted_iota(jnp.int32, (16, CHUNK), 0) == 0
    v_cols[HD:, :] = jnp.where(ones_row, 1.0, 0.0).astype(BF16)

    for i in range(1, HEADS):
        slab_link(i).wait_recv()
    own = PLACE[(0, 0)]
    slabs = [slab_out[0].astype(F32)] + [slab_in[i].astype(F32) for i in range(1, HEADS)]
    for i in range(2):
        pieces = [slab[i * SLAB : (i + 1) * SLAB, :] for slab in slabs]
        kv[i, own : own + BLOCK, :] = jnp.concatenate(pieces, axis=0).astype(BF16)
    core_link((0, 0)).start()
    for dy in (1, 3):
        y_link(0, dy).start()
    x_link().start()
    y_link(0, 2).start()

    def turn(chunk):
        rows = key_rows(chunk)
        v_cols[:HD, :] = kv[1, rows, :].T

    def forward(chunk, masked, middle):
        rows = key_rows(chunk)

        def scores(g):
            s = dot(kv[0, rows, :], q_cols[g])
            if masked:
                s = s + scaled[:, :ROWS].astype(F32)
            wide[g % WIDE] = s
            earlier = run_max[g : g + 1, :]
            largest = jnp.maximum(earlier, jnp.max(s, axis=0, keepdims=True))
            run_max[g : g + 1, :] = largest
            chunk_max[chunk, g : g + 1, :] = largest
            return jnp.exp2((earlier - largest) * EXP2_SCALE)

        def output(g, shrink):
            columns = slice(g * ROWS, (g + 1) * ROWS)
            largest = chunk_max[chunk, g : g + 1, :]
            w = jnp.exp2((wide[g % WIDE] - largest) * EXP2_SCALE).astype(BF16)
            weights[rows, columns] = w
            acc[g] = acc[g] * shrink + dot(v_cols[...], weights[rows, columns])

        for first in range(0, GROUP, WIDE):
            some = range(first, first + WIDE)
            shrinks = [scores(g) for g in some]
            middle(first // WIDE)

            @pl.when(seq >= 0)
            def _():
                for g, shrink in zip(some, shrinks):
                    output(g, shrink)

    def during_near(half):
        if half == 0:
            y_link(0, 3).wait_recv()
            core_link((0, 3)).start()
            core_link((1, 0)).start()
        else:
            y_link(0, 2).wait_recv()
            core_link((0, 2)).start()

    def during_far(half):
        if half == 1:
            for d in (2, 4):

                @pl.when(seq >= d)
                def _():
                    resp_link(d).wait_recv()

                @pl.when(seq < d)
                def _():
                    first = (SPAN - d) * ROWS
                    kv[:, first : first + ROWS, :] = jnp.zeros((2, ROWS, HD), BF16)

            for d in (1, 3):
                core_resp_link(d).start()

    def during_resp(half):
        if half == 0:
            for dy in (1, 3):
                y_link(1, dy).wait_recv()
                core_link((1, dy)).start()

    y_link(0, 1).wait_recv()
    core_link((0, 1)).start()
    x_link().wait_recv()
    for dy in (1, 3, 2):
        y_link(1, dy).start()
    core_link((0, 0)).wait_recv()
    core_link((0, 1)).wait_recv()
    turn(1)
    forward(1, False, during_near)

    core_link((0, 3)).wait_recv()
    core_link((0, 2)).wait_recv()
    turn(2)
    forward(2, False, during_far)

    for d in (1, 3):
        core_resp_link(d).wait_recv()
    turn(0)
    forward(0, True, during_resp)

    def prompt_chunk(chunk, carry):
        @pl.when(chunk == 3)
        def _():
            core_link((1, 0)).wait_recv()
            core_link((1, 1)).wait_recv()

        @pl.when(chunk == 4)
        def _():
            core_link((1, 3)).wait_recv()
            core_link((1, 2)).wait_recv()

        def during(half):
            if half == 0:

                @pl.when(chunk == 3)
                def _():
                    y_link(1, 2).wait_recv()
                    core_link((1, 2)).start()

        turn(chunk)
        forward(chunk, False, during)
        return carry

    lax.fori_loop(3, CHUNKS, prompt_chunk, 0)

    for g in range(GROUP):
        inverse = 1.0 / acc[g, HD : HD + 1, :]
        rounded = (acc[g, :HD, :] * inverse).astype(BF16)
        scaled[:ROWS, g * HD : (g + 1) * HD] = rounded.T
        products = cot_cols[g, :HD, :].astype(F32) * rounded.astype(F32)
        rest = -jnp.sum(products, axis=0, keepdims=True)
        for i in range(3):
            piece = rest.astype(BF16)
            cot_cols[g, HD + i : HD + i + 1, :] = piece
            rest = rest - piece.astype(F32)
        for chunk in range(CHUNKS):
            chunk_max[chunk, g : g + 1, :] = inverse * jnp.exp2(
                (chunk_max[chunk, g : g + 1, :] - run_max[g : g + 1, :]) * EXP2_SCALE
            )

    out_copy = pltpu.make_async_copy(
        scaled.at[pl.ds(0, ROWS), pl.ds(0, GROUP * HD)], out_ref, local_sem.at[2 + 2 * GROUP]
    )
    out_copy.start()
    is_one = lax.broadcasted_iota(jnp.int32, (CHUNK, HD), 1) < 3
    ones_columns = jnp.where(is_one, 1.0, 0.0).astype(BF16)

    def pair_sum(chip):
        core_back(chip).wait_recv()
        row = PLACE[chip]
        half = (row - CHUNK) // 2
        partial[:, row : row + BLOCK, :] = (
            partial[:, row : row + BLOCK, :] + from_core[:, half : half + BLOCK, :]
        )

    def sum_over_y():
        place = PLACE[(1, 0)]
        total = partial[:, place : place + BLOCK, :].astype(F32)
        for dy in (1, 2, 3):
            y_back(1, dy).wait_recv()
            total = total + from_y[1, dy - 1].astype(F32)
        partial[:, place : place + BLOCK, :] = total.astype(BF16)
        x_back().start()

    def backward(chunk, middle=None):
        rows = key_rows(chunk)
        k_cols[:, rows] = kv[0, rows, :].T
        values = jnp.concatenate([kv[1, rows, :], ones_columns], axis=1)
        for g in range(GROUP):
            columns = slice(g * ROWS, (g + 1) * ROWS)
            wide[g % WIDE] = dot(values, cot_cols[g])
            w = weights[rows, columns].astype(F32) * chunk_max[chunk, g : g + 1, :]
            scaled[:, columns] = w.astype(BF16)
            weights[rows, columns] = (w * wide[g % WIDE]).astype(BF16)
        if middle is not None:
            middle()
        partial[1, rows, :] = dot(scaled[...], cot_rows[...]).astype(BF16)
        partial[0, rows, :] = (dot(weights[rows, :], q_rows[...]) * SCALE).astype(BF16)

    def pass_back(chunk):
        for chip in CHIPS[chunk]:
            pair_sum(chip)
            if chip[1] != 0:
                y_back(*chip).start()

    def prompt_back(step, carry):
        chunk = CHUNKS - 1 - step
        for later in (1, 2):

            @pl.when(chunk == later)
            def _():
                pass_back(later + 2)

        backward(chunk)
        for done in (4, 3, 2, 1):

            @pl.when(chunk == done)
            def _():
                for chip in CHIPS[done]:
                    core_back(chip).start()

        return carry

    out_copy.wait()
    lax.fori_loop(0, CHUNKS - 1, prompt_back, 0)
    pass_back(2)

    def last_sums():
        @pl.when(seq >= 0)
        def _():
            pass_back(1)
            sum_over_y()

    backward(0, last_sums)

    for d in (1, 3):
        core_resp_back(d).start()

    def grad_query(g):
        turned = dot(k_cols[...], weights[:, g * ROWS : (g + 1) * ROWS]) * SCALE
        grad_q_ref[:, g * HD : (g + 1) * HD] = turned.astype(BF16).T

    for g in range(2):
        grad_query(g)

    for d in (1, 3):
        core_resp_back(d).wait_recv()
        near = pl.ds(pl.multiple_of((SPAN - (2 * core + d - 1)) * ROWS, ROWS), ROWS)
        partial[:, near, :] = partial[:, near, :] + from_core_resp[d // 2]
    for d in (4, 2):

        @pl.when(seq >= d)
        def _():
            resp_back(d).start()

    for g in range(2, 6):
        grad_query(g)

    total = partial[:, own : own + BLOCK, :].astype(F32)
    for dy in (1, 2, 3):
        y_back(0, dy).wait_recv()
        total = total + from_y[0, dy - 1].astype(F32)
    x_back().wait_recv()
    total = total + from_x[...].astype(F32)
    for i in range(HEADS):
        two = [total[j, i * SLAB : (i + 1) * SLAB, :] for j in range(2)]
        back_out[i] = jnp.concatenate(two, axis=0).astype(BF16)
    for i in range(1, HEADS):
        slab_back(i).start()

    for g in range(6, GROUP):
        grad_query(g)

    total = partial[:, SPAN * ROWS : CHUNK, :].astype(F32)
    for d in (2, 4):

        @pl.when(seq + d < 16)
        def _():
            resp_back(d).wait_recv()

        @pl.when(seq + d >= 16)
        def _():
            from_resp[d // 2 - 1] = jnp.zeros((2, ROWS, HD), BF16)

        total = total + from_resp[d // 2 - 1].astype(F32)
    grad_k_resp[...] = total[0].astype(BF16)
    grad_v_resp[...] = total[1].astype(BF16)

    for i in range(HEADS):
        if i > 0:
            slab_back(i).wait_recv()
        source = back_out if i == 0 else back_in
        slab = source[i].astype(F32)
        columns = pl.ds(pl.multiple_of(((head + i) % HEADS) * HD, HD), HD)
        grad_k_prompt[:, columns] = slab[:SLAB, :].astype(BF16)
        grad_v_prompt[:, columns] = slab[SLAB:, :].astype(BF16)

    for i in range(1, HEADS):
        slab_link(i).wait_send()
        slab_back(i).wait_send()
    for d in (2, 4):

        @pl.when(seq + d < 16)
        def _():
            resp_link(d).wait_send()

        @pl.when(seq >= d)
        def _():
            resp_back(d).wait_send()

    for d in (1, 3):
        core_resp_link(d).wait_send()
        core_resp_back(d).wait_send()
    for chip in PLACE:
        core_link(chip).wait_send()
        core_back(chip).wait_send()
        if chip[1] != 0:
            y_link(*chip).wait_send()
            y_back(*chip).wait_send()
    x_link().wait_send()
    x_back().wait_send()


def write_out(*refs):
    sources, targets, held, sems = refs[:6], refs[6:12], refs[12:18], refs[18]
    loads = [pltpu.make_async_copy(sources[i], held[i], sems.at[i]) for i in range(6)]
    stores = [pltpu.make_async_copy(held[i], targets[i], sems.at[6 + i]) for i in range(6)]
    for load in loads:
        load.start()
    for load, store in zip(loads, stores):
        load.wait()
        store.start()
    for store in stores:
        store.wait()


def shards(prompt_k, prompt_v, resp_q, resp_k, resp_v, grad_out, resp_lengths):
    vmem = pl.BlockSpec(memory_space=pltpu.VMEM)
    anywhere = pl.BlockSpec(memory_space=pl.ANY)
    links = 2 * (HEADS - 1) + 2 * 4 + 2 * (6 + 1 + 8)
    like = jax.ShapeDtypeStruct
    results = pl.pallas_call(
        kernel,
        out_shape=(
            like((ROWS, GROUP * HD), BF16),
            like((ROWS, GROUP * HD), BF16),
            like((ROWS, HD), BF16),
            like((ROWS, HD), BF16),
            like((SLAB, HEADS * HD), BF16),
            like((SLAB, HEADS * HD), BF16),
        ),
        in_specs=[pl.BlockSpec(memory_space=pltpu.SMEM), vmem, vmem] + [anywhere] * 4,
        out_specs=[anywhere] + [vmem] * 5,
        scratch_shapes=[
            pltpu.VMEM((2, KEYS, HD), BF16),
            pltpu.VMEM((HD, KEYS), BF16),
            pltpu.VMEM((HD + 16, CHUNK), BF16),
            pltpu.VMEM((GROUP, HD, ROWS), BF16),
            pltpu.VMEM((GROUP * ROWS, HD), BF16),
            pltpu.VMEM((GROUP, 2 * HD, ROWS), BF16),
            pltpu.VMEM((GROUP * ROWS, HD), BF16),
            pltpu.VMEM((KEYS, GROUP * ROWS), BF16),
            pltpu.VMEM((CHUNK, GROUP * ROWS), BF16),
            pltpu.VMEM((WIDE, CHUNK, ROWS), F32),
            pltpu.VMEM((GROUP, ROWS), F32),
            pltpu.VMEM((CHUNKS, GROUP, ROWS), F32),
            pltpu.VMEM((GROUP, HD + 16, ROWS), F32),
            pltpu.VMEM((HEADS, 2 * SLAB, HD), BF16),
            pltpu.VMEM((HEADS, 2 * SLAB, HD), BF16),
            pltpu.VMEM((2, KEYS, HD), BF16),
            pltpu.VMEM((2, 8 * BLOCK, HD), BF16),
            pltpu.VMEM((2, 3, 2, BLOCK, HD), BF16),
            pltpu.VMEM((2, BLOCK, HD), BF16),
            pltpu.VMEM((2, 2, ROWS, HD), BF16),
            pltpu.VMEM((2, 2, ROWS, HD), BF16),
            pltpu.VMEM((HEADS, 2 * SLAB, HD), BF16),
            pltpu.VMEM((HEADS, 2 * SLAB, HD), BF16),
            pltpu.SemaphoreType.DMA((3 + 2 * GROUP,)),
            pltpu.SemaphoreType.DMA((links,)),
            pltpu.SemaphoreType.DMA((links,)),
        ],
        compiler_params=pltpu.CompilerParams(
            collective_id=0, has_side_effects=True, vmem_limit_bytes=63 * 2**20
        ),
        cost_estimate=pl.CostEstimate(
            flops=12 * ROWS * GROUP * KEYS * HD,
            bytes_accessed=4 * 2**20,
            transcendentals=ROWS * GROUP * KEYS,
        ),
        name="shared_prompt_attention",
    )(resp_lengths, prompt_k, prompt_v, resp_q, resp_k, resp_v, grad_out)
    return pl.pallas_call(
        write_out,
        out_shape=tuple(like(r.shape, r.dtype) for r in results),
        in_specs=[anywhere] * 6,
        out_specs=[anywhere] * 6,
        scratch_shapes=[pltpu.VMEM(r.shape, r.dtype) for r in results]
        + [pltpu.SemaphoreType.DMA((12,))],
        name="write_out",
    )(*results)


def solution(mesh):
    placed = (
        P(("seq", "head"), None),
        P(("seq", "head"), None),
        P("seq", "head"),
        P("seq", "head"),
        P("seq", "head"),
        P("seq", "head"),
        P(),
    )
    return jax.shard_map(
        shards,
        mesh=mesh,
        in_specs=placed,
        out_specs=(
            P("seq", "head"),
            P("seq", "head"),
            P("seq", "head"),
            P("seq", "head"),
            P(("seq", "head"), None),
            P(("seq", "head"), None),
        ),
        check_vma=False,
    )
```
